128 devices in a mesh: fsdp: 32 (over z, y_hi, x), tp: 4 (over y_lo, core).
Axes of the slice: x: 4, y: 4 (y_hi: 2, y_lo: 2; y = y_hi * 2 + y_lo), z: 4, core: 2. Of those that a mesh axis runs over, the one named last changes fastest.
Arguments:
- inputs: bfloat16 [4, 64, 2560], P(None, 'fsdp'), may hold values from -6 to 6
- norm_gain: bfloat16 [2, 2560], replicated, may hold values from 0.099609375 to 1.8984375
- old_wq: bfloat16 [2, 2560, 4096], P(None, None, 'tp'), may hold values from -0.125 to 0.125
- old_wk: bfloat16 [2, 2560, 512], P(None, None, 'tp'), may hold values from -0.125 to 0.125
- old_wv: bfloat16 [2, 2560, 512], P(None, None, 'tp'), may hold values from -0.125 to 0.125
- old_wo: bfloat16 [2, 2560, 4096], P(None, None, 'tp'), may hold values from -0.09375 to 0.09375
- new_wq: bfloat16 [2, 2560, 4096], P(None, ('fsdp', 'tp')), may hold values from -0.125 to 0.125
- new_wk: bfloat16 [2, 2560, 512], P(None, ('fsdp', 'tp')), may hold values from -0.125 to 0.125
- new_wv: bfloat16 [2, 2560, 512], P(None, ('fsdp', 'tp')), may hold values from -0.125 to 0.125
- new_wo: bfloat16 [2, 2560, 4096], P(None, ('fsdp', 'tp')), may hold values from -0.09375 to 0.09375
- cache_keys: bfloat16 [2, 64, 256, 512], P(None, 'fsdp', None, 'tp'), may hold values from -120 to 120
- cache_values: bfloat16 [2, 64, 256, 512], P(None, 'fsdp', None, 'tp'), may hold values from -6 to 6
- cache_lengths: int32 [64], P('fsdp'), may hold values from 1 to 256, as said below
- refresh_bound: int32 [4], replicated, may hold values from 0 to 2, as said below
Outputs:
- stream_out: float32 [4, 64, 2560], P(None, 'fsdp')
The draws below stay inside these ranges and needn't reach their ends.
Inputs may be any that keep to these rules, and one draw needn't show every extreme that they name: `cache_lengths`: some row has exactly 256 live slots. `refresh_bound`: never falls from step to step; it is 2 at the last step.
All inputs are finite; a program needn't handle non-finite values.
Results may differ from the reference program's by a relative error of at most 0.015.
Values may be sent and summed in bfloat16 or wider, within the bound.
A program may use at most 384 MiB of HBM per device.

```python
import math
import jax
import jax.numpy as jnp
from jax import lax

D = 2560
QH = 32
KVH = 4
HD = 128
QB = 128
LAYERS = 2
STEPS = 4
CTX = 256
ROWS = 64


def draw_cache_lengths(key, part):
    key = jax.random.fold_in(key, 11)
    key_len, key_row = jax.random.split(key)
    drawn_lengths = jax.random.randint(key_len, (ROWS,), 1, CTX + 1)
    long_row = jax.random.randint(key_row, (), 0, ROWS)
    return jnp.where(jnp.arange(ROWS) == long_row, CTX, drawn_lengths).astype(jnp.int32)


def draw_refresh_bound(key, part):
    key = jax.random.fold_in(key, 29)
    sorted_draw = jnp.sort(jax.random.randint(key, (STEPS,), 0, LAYERS + 1))
    position = jnp.arange(STEPS)
    return jnp.where(position == STEPS - 1, LAYERS, sorted_draw).astype(jnp.int32)


def draw_cache_keys(key, part):
    key = jax.random.fold_in(key, 13)
    key_drawn = jax.random.fold_in(key, 0)
    drawn_keys = jnp.clip(jax.random.normal(key_drawn, (LAYERS, ROWS, CTX, KVH * HD), jnp.float32), -5.0, 5.0)
    return drawn_keys.astype(jnp.bfloat16)


def block_levels(rng, shape, pieces, low, largest):
    def one(dim, parts):
        draws = jax.random.uniform(jax.random.fold_in(jax.random.fold_in(rng, 6), dim), (parts,), jnp.float32, low / len(pieces), largest / len(pieces))
        return jnp.repeat(jnp.exp(draws), shape[dim] // parts).reshape((-1,) + (1,) * (len(shape) - dim - 1))

    loudness = one(*pieces[0])
    for cut in pieces[1:]:
        loudness = loudness * one(*cut)
    return loudness


def bell_draw(rng, shape, width, bound, cuts=(), kind=jnp.bfloat16):
    values = jax.random.normal(rng, shape, jnp.float32) * width
    if len(cuts) > 0:
        values = block_levels(rng, shape, cuts, -0.22, 0.18) * values
    return jnp.clip(values, min=-bound, max=bound).astype(kind)


def setup_inputs(seed: int = 0) -> dict:
    splits = jax.random.split(jax.random.key(seed), 15)
    return {
        "inputs": bell_draw(splits[0], (STEPS, ROWS, D), 1.0, 6.0, ((1, 32),)),
        "norm_gain": jnp.clip(1.0 + 0.18 * jax.random.normal(splits[1], (LAYERS, D), jnp.float32), 0.099609375, 1.8984375).astype(jnp.bfloat16),
        "old_wq": bell_draw(splits[2], (LAYERS, D, QH * HD), D ** -0.5, 0.125, ((2, 4),)),
        "old_wk": bell_draw(splits[3], (LAYERS, D, KVH * HD), D ** -0.5, 0.125, ((2, 4),)),
        "old_wv": bell_draw(splits[4], (LAYERS, D, KVH * HD), D ** -0.5, 0.125, ((2, 4),)),
        "old_wo": bell_draw(splits[5], (LAYERS, D, QH * HD), (QH * HD) ** -0.5, 0.09375, ((2, 4),)),
        "new_wq": bell_draw(splits[6], (LAYERS, D, QH * HD), D ** -0.5, 0.125, ((1, 128),)),
        "new_wk": bell_draw(splits[7], (LAYERS, D, KVH * HD), D ** -0.5, 0.125, ((1, 128),)),
        "new_wv": bell_draw(splits[8], (LAYERS, D, KVH * HD), D ** -0.5, 0.125, ((1, 128),)),
        "new_wo": bell_draw(splits[9], (LAYERS, D, QH * HD), (QH * HD) ** -0.5, 0.09375, ((1, 128),)),
        "cache_keys": draw_cache_keys(jax.random.fold_in(splits[14], 71), 0),
        "cache_values": bell_draw(splits[11], (LAYERS, ROWS, CTX, KVH * HD), 1.0, 6.0, ((1, 32), (3, 4))),
        "cache_lengths": draw_cache_lengths(jax.random.fold_in(splits[14], 71), 0),
        "refresh_bound": draw_refresh_bound(jax.random.fold_in(splits[14], 71), 0),
    }


def to_grid(values):
    magnitude = jnp.abs(values)
    exponent = jnp.floor(jnp.log2(jnp.maximum(magnitude, 2.0 ** (-6))))
    spacing = jnp.exp2(exponent - 3.0)
    return jnp.sign(values) * jnp.floor(magnitude / spacing + 0.5) * spacing

def block_scales(weight):
    layer_count, row_count, col_count = weight.shape
    tile_view = jnp.abs(weight).reshape(layer_count, row_count // QB, QB, col_count // QB, QB)
    peak_table = lax.optimization_barrier(jnp.max(tile_view, axis=(2, 4))).astype(jnp.float32)
    scales = (peak_table + 1e-06) / 448.0
    return jnp.repeat(jnp.repeat(scales, QB, axis=1), QB, axis=2)

def refresh(weight):
    scales = block_scales(weight)
    encoded = to_grid(weight.astype(jnp.float32) / scales).astype(jnp.bfloat16)
    encoded = lax.optimization_barrier(encoded)
    return (encoded.astype(jnp.float32) * scales).astype(jnp.bfloat16)

def normed(hidden, gain):
    mean_square = lax.optimization_barrier(jnp.mean(hidden * hidden, axis=-1, keepdims=True))
    return (hidden * lax.rsqrt(mean_square + 1e-06) * gain.astype(jnp.float32)).astype(jnp.bfloat16)

def attend(queries, cache_k, cache_v, fresh_k, fresh_v, lengths):
    row_count = queries.shape[0]
    kv_heads = cache_k.shape[-1] // HD
    group_size = queries.shape[-1] // (kv_heads * HD)
    score_scale = 1.0 / math.sqrt(HD)
    query_view = queries.astype(jnp.float32).reshape(row_count, kv_heads, group_size, HD)
    key_view = cache_k.astype(jnp.float32).reshape(row_count, -1, kv_heads, HD)
    value_view = cache_v.astype(jnp.float32).reshape(row_count, -1, kv_heads, HD)
    fresh_key_view = fresh_k.astype(jnp.float32).reshape(row_count, -1, kv_heads, HD)
    fresh_value_view = fresh_v.astype(jnp.float32).reshape(row_count, -1, kv_heads, HD)
    score_old = jnp.einsum('rkgd,rckd->rkgc', query_view, key_view) * score_scale
    live_mask = jnp.arange(key_view.shape[1])[None, :] < lengths[:, None]
    score_old = jnp.where(live_mask[:, None, None, :], score_old, -1e+30)
    score_new = jnp.einsum('rkgd,rskd->rkgs', query_view, fresh_key_view) * score_scale
    peak_score = jnp.maximum(lax.optimization_barrier(jnp.max(score_old, axis=3)), lax.optimization_barrier(jnp.max(score_new, axis=3)))
    prob_old = jnp.exp(score_old - peak_score[..., None])
    prob_new = jnp.exp(score_new - peak_score[..., None])
    denom_sum = lax.optimization_barrier(jnp.sum(prob_old, axis=3)) + lax.optimization_barrier(jnp.sum(prob_new, axis=3))
    rounded_old = lax.optimization_barrier(prob_old.astype(jnp.bfloat16)).astype(jnp.float32)
    rounded_new = lax.optimization_barrier(prob_new.astype(jnp.bfloat16)).astype(jnp.float32)
    weighted = jnp.einsum('rkgc,rckd->rkgd', rounded_old, value_view)
    weighted = weighted + jnp.einsum('rkgs,rskd->rkgd', rounded_new, fresh_value_view)
    return (weighted / denom_sum[..., None]).reshape(row_count, -1).astype(jnp.bfloat16)

def reference(inputs, norm_gain, old_wq, old_wk, old_wv, old_wo, new_wq, new_wk, new_wv, new_wo, cache_keys, cache_values, cache_lengths, refresh_bound):
    fresh_set = [refresh(matrix) for matrix in (new_wq, new_wk, new_wv, new_wo)]
    stale_set = [old_wq, old_wk, old_wv, old_wo]
    step_keys = [[] for layer_idx in range(LAYERS)]
    step_values = [[] for layer_idx in range(LAYERS)]
    step_outputs = []
    for step_idx in range(STEPS):
        hidden = inputs[step_idx].astype(jnp.float32)
        for layer_idx in range(LAYERS):
            use_new = layer_idx < refresh_bound[step_idx]
            w_query, w_key, w_value, w_out = [jnp.where(use_new, fresh[layer_idx], stale[layer_idx]) for fresh, stale in zip(fresh_set, stale_set)]
            normed_x = normed(hidden, norm_gain[layer_idx])
            queries = jnp.dot(normed_x, w_query, preferred_element_type=jnp.float32).astype(jnp.bfloat16)
            key_now = jnp.dot(normed_x, w_key, preferred_element_type=jnp.float32).astype(jnp.bfloat16)
            value_now = jnp.dot(normed_x, w_value, preferred_element_type=jnp.float32).astype(jnp.bfloat16)
            step_keys[layer_idx].append(key_now)
            step_values[layer_idx].append(value_now)
            attended = attend(queries, cache_keys[layer_idx], cache_values[layer_idx], jnp.stack(step_keys[layer_idx], axis=1), jnp.stack(step_values[layer_idx], axis=1), cache_lengths)
            hidden = hidden + lax.dot_general(attended, w_out, (((1,), (1,)), ((), ())), preferred_element_type=jnp.float32)
        step_outputs.append(hidden)
    return jnp.stack(step_outputs)
```

```python
import math

import jax
import jax.numpy as jnp
from jax import lax
from jax.sharding import PartitionSpec as P

D = 2560
HD = 128
QB = 128
LAYERS = 2
STEPS = 4
GROUPS = 4
REPLICAS = 32
WORLD = GROUPS * REPLICAS


def to_grid(values):
    magnitude = jnp.abs(values)
    exponent = jnp.floor(jnp.log2(jnp.maximum(magnitude, 2.0 ** (-6))))
    spacing = jnp.exp2(exponent - 3.0)
    return jnp.sign(values) * jnp.floor(magnitude / spacing + 0.5) * spacing


def partial_peaks(weight, row_start):
    layer_count, row_count, col_count = weight.shape
    col_peaks = jnp.max(
        jnp.abs(weight).reshape(layer_count, row_count, col_count // QB, QB), axis=3
    ).astype(jnp.float32)
    row_block = (row_start + jnp.arange(row_count)) // QB
    in_block = row_block[:, None] == jnp.arange(D // QB)[None, :]
    return jnp.max(jnp.where(in_block[None, :, :, None], col_peaks[:, :, None, :], 0.0), axis=1)


def refresh(weight, peak_table, row_start):
    layer_count, row_count, col_count = weight.shape
    scales = (peak_table + 1e-06) / 448.0
    row_block = (row_start + jnp.arange(row_count)) // QB
    scales = jnp.take(scales, row_block, axis=1)[..., None]
    blocked = weight.astype(jnp.float32).reshape(layer_count, row_count, col_count // QB, QB)
    coded = to_grid(blocked / scales)
    return (coded * scales).astype(jnp.bfloat16).reshape(layer_count, row_count, col_count)


def normed(hidden, gain):
    mean_square = jnp.mean(hidden * hidden, axis=-1, keepdims=True)
    return (hidden * lax.rsqrt(mean_square + 1e-06) * gain.astype(jnp.float32)).astype(jnp.bfloat16)


def attend(queries, cache_k, cache_v, step_k, step_v, lengths):
    rows = cache_k.shape[0]
    score_scale = 1.0 / math.sqrt(HD)
    query = queries.reshape(STEPS, rows, 8, HD)
    old = jnp.einsum("srgd,rcd->srgc", query, cache_k, preferred_element_type=jnp.float32)
    live = jnp.arange(cache_k.shape[1])[None, :] < lengths[:, None]
    old = jnp.where(live[None, :, None, :], old * score_scale, -1e30)
    new = jnp.einsum("srgd,urd->srgu", query, step_k, preferred_element_type=jnp.float32)
    seen = jnp.arange(STEPS)[None, :] <= jnp.arange(STEPS)[:, None]
    new = jnp.where(seen[:, None, None, :], new * score_scale, -1e30)
    peak = jnp.maximum(jnp.max(old, axis=3), jnp.max(new, axis=3))[..., None]
    prob_old = jnp.exp(old - peak)
    prob_new = jnp.exp(new - peak)
    total = jnp.sum(prob_old, axis=3) + jnp.sum(prob_new, axis=3)
    weighted = jnp.einsum(
        "srgc,rcd->srgd",
        prob_old.astype(jnp.bfloat16),
        cache_v,
        preferred_element_type=jnp.float32,
    )
    weighted = weighted + jnp.einsum(
        "srgu,urd->srgd",
        prob_new.astype(jnp.bfloat16),
        step_v,
        preferred_element_type=jnp.float32,
    )
    return (weighted / total[..., None]).astype(jnp.bfloat16).reshape(STEPS, rows, 8 * HD)


def on_device(
    inputs,
    norm_gain,
    old_wq,
    old_wk,
    old_wv,
    old_wo,
    new_wq,
    new_wk,
    new_wv,
    new_wo,
    cache_keys,
    cache_values,
    cache_lengths,
    refresh_bound,
):
    replica = lax.axis_index("fsdp")
    row_start = lax.axis_index(("fsdp", "tp")) * new_wq.shape[1]
    trained = jnp.concatenate([new_wq, new_wk, new_wv, new_wo], axis=2)
    peaks = lax.pmax(partial_peaks(trained, row_start), ("fsdp", "tp"))
    fresh = refresh(trained, peaks, row_start)
    fresh_q, fresh_k, fresh_v, fresh_o = jnp.split(fresh, (4096, 4608, 5120), axis=2)

    def by_destination(matrix):
        each = matrix.shape[2] // WORLD
        cut = matrix.reshape(LAYERS, 20, GROUPS, REPLICAS, each)
        return cut.transpose(3, 2, 0, 1, 4).reshape(WORLD, LAYERS, 20, each)

    moving = jnp.concatenate([by_destination(m) for m in (fresh_q, fresh_k, fresh_v)], axis=3)
    landed = lax.all_to_all(moving, ("fsdp", "tp"), split_axis=0, concat_axis=0, tiled=True)
    fresh_in = landed.transpose(1, 0, 2, 3).reshape(LAYERS, D, 40)
    moving = fresh_o.reshape(LAYERS, 20, GROUPS, 1024).transpose(2, 0, 1, 3)
    landed = lax.all_to_all(moving, "tp", split_axis=0, concat_axis=0, tiled=True)
    fresh_out = landed.transpose(1, 0, 2, 3).reshape(LAYERS, 80, 1024)

    def own_columns(matrix):
        each = matrix.shape[2] // REPLICAS
        return lax.dynamic_slice_in_dim(matrix, replica * each, each, 2)

    stale_in = jnp.concatenate([own_columns(m) for m in (old_wq, old_wk, old_wv)], axis=2)
    stale_out = lax.dynamic_slice_in_dim(old_wo, replica * 80, 80, 1)

    hidden = inputs.astype(jnp.float32)
    rows = hidden.shape[1]
    for layer in range(LAYERS):
        use_new = (layer < refresh_bound)[None, :, None, None]
        normed_x = normed(hidden, norm_gain[layer])
        everyone = lax.all_gather(normed_x, "fsdp", axis=0)
        both = jnp.concatenate([fresh_in[layer], stale_in[layer]], axis=1)
        product = jnp.einsum("fsrd,de->fsre", everyone, both, preferred_element_type=jnp.float32)
        product = product.astype(jnp.bfloat16)
        product = jnp.where(use_new, product[..., :40], product[..., 40:])
        mine = lax.all_to_all(product, "fsdp", split_axis=0, concat_axis=0, tiled=True)
        mine = mine.transpose(1, 2, 0, 3)
        queries = mine[..., :32].reshape(STEPS, rows, 1024)
        step_k = mine[..., 32:36].reshape(STEPS, rows, HD)
        step_v = mine[..., 36:].reshape(STEPS, rows, HD)
        attended = attend(
            queries, cache_keys[layer], cache_values[layer], step_k, step_v, cache_lengths
        )
        everyone = lax.all_gather(attended, "fsdp", axis=0)
        both = jnp.concatenate([fresh_out[layer], stale_out[layer]], axis=0)
        product = jnp.einsum("fsrd,ed->fsre", everyone, both, preferred_element_type=jnp.float32)
        product = jnp.where(use_new, product[..., :80], product[..., 80:])
        mine = lax.all_to_all(product, "fsdp", split_axis=0, concat_axis=0, tiled=True)
        mine = mine.transpose(1, 2, 0, 3).reshape(STEPS, rows, D)
        hidden = hidden + lax.psum(mine, "tp")
    return hidden


def solution(mesh):
    in_specs = (
        P(None, "fsdp", None),
        P(),
        P(None, None, "tp"),
        P(None, None, "tp"),
        P(None, None, "tp"),
        P(None, None, "tp"),
        P(None, ("fsdp", "tp"), None),
        P(None, ("fsdp", "tp"), None),
        P(None, ("fsdp", "tp"), None),
        P(None, ("fsdp", "tp"), None),
        P(None, "fsdp", None, "tp"),
        P(None, "fsdp", None, "tp"),
        P("fsdp"),
        P(),
    )
    out_specs = P(None, "fsdp", None)
    return jax.shard_map(
        on_device, mesh=mesh, in_specs=in_specs, out_specs=out_specs, check_vma=False
    )
```

```python
import functools
import math

import jax
import jax.numpy as jnp
from jax import lax
from jax.experimental import pallas as pl
from jax.experimental.pallas import tpu as pltpu
from jax.sharding import PartitionSpec as P

MESH = pl.DeviceIdType.MESH
D = 2560
HD = 128
STEPS = 4
OWNERS = 32
KEEP = 20
PART = 640
HALF = 512
ROWS = 256


def use_new_rows(bound_ref, layer, row_count):
    step = lax.rem(lax.broadcasted_iota(jnp.int32, (row_count, 1), 0), 8) // 2
    bound = jnp.where(
        step == 0,
        bound_ref[0],
        jnp.where(step == 1, bound_ref[1], jnp.where(step == 2, bound_ref[2], bound_ref[3])),
    )
    return layer < bound


def refresh_block(block):
    peak = jnp.max(jnp.abs(block), axis=(0, 1), keepdims=True)
    scale = (peak + 1e-06) / 448.0
    value = block / scale
    magnitude = jnp.abs(value)
    exponent = jnp.floor(jnp.log2(jnp.maximum(magnitude, 2.0 ** (-6))))
    coded = jnp.floor(magnitude * jnp.exp2(3.0 - exponent) + 0.5) * jnp.exp2(exponent - 3.0)
    coded = jnp.where(value < 0.0, -coded, coded).astype(jnp.bfloat16).astype(jnp.float32)
    return (coded * scale).astype(jnp.bfloat16)


def attend(sums, keys, values, length_ref):
    score_scale = 1.0 / math.sqrt(HD)
    queries = jnp.concatenate(
        [sums[g][:, HD * h : HD * h + HD] for g in range(2) for h in range(4)], axis=0
    ).astype(jnp.bfloat16)
    step_k = sums[0][:, HALF:PART].astype(jnp.bfloat16)
    step_v = sums[1][:, HALF:PART].astype(jnp.bfloat16)
    nt = (((1,), (1,)), ((), ()))
    old = lax.dot_general(queries, keys, nt, preferred_element_type=jnp.float32) * score_scale
    new = lax.dot_general(queries, step_k, nt, preferred_element_type=jnp.float32) * score_scale
    row = lax.broadcasted_iota(jnp.int32, (64, 512), 0)
    col = lax.broadcasted_iota(jnp.int32, (64, 512), 1)
    same = lax.rem(row, 2) == col // 256
    length = jnp.where(col // 256 == 0, length_ref[0], length_ref[1])
    old = jnp.where(same & (lax.rem(col, 256) < length), old, -1e30)
    row = lax.broadcasted_iota(jnp.int32, (64, 8), 0)
    col = lax.broadcasted_iota(jnp.int32, (64, 8), 1)
    same = lax.rem(row, 2) == lax.rem(col, 2)
    new = jnp.where(same & (col // 2 <= lax.rem(row, 8) // 2), new, -1e30)
    peak = jnp.maximum(
        jnp.max(old, axis=1, keepdims=True), jnp.max(new, axis=1, keepdims=True)
    )
    old = jnp.exp(old - peak)
    new = jnp.exp(new - peak)
    total = jnp.sum(old, axis=1, keepdims=True) + jnp.sum(new, axis=1, keepdims=True)
    mixed = jnp.dot(old.astype(jnp.bfloat16), values, preferred_element_type=jnp.float32)
    mixed = mixed + jnp.dot(new.astype(jnp.bfloat16), step_v, preferred_element_type=jnp.float32)
    return (mixed / total).astype(jnp.bfloat16)


def kernel(
    x0_ref,
    xr_ref,
    gain_ref,
    length_ref,
    bound_ref,
    old_wq,
    old_wk,
    old_wv,
    old_wo,
    new_wq,
    new_wk,
    new_wv,
    new_wo,
    cache_k,
    cache_v,
    out_ref,
    slabs,
    raw,
    fresh,
    stale,
    keys,
    values,
    x_land,
    r_land,
    product,
    b0_land,
    b1_land,
    att,
    d_land,
    e_land,
    ag_land,
    h_keep,
    h_land,
    f_land,
    f_keep,
    o_land,
    w_send,
    x_send,
    r_send,
    b_send,
    d_send,
    e_send,
    ag_send,
    h_send,
    f_send,
    o_send,
    w_recv,
    own_sem,
    local_sem,
    x_recv,
    r_recv,
    b_recv,
    d_recv,
    e_recv,
    ag_recv,
    h_recv,
    f_recv,
    o_recv,
):
    f = lax.axis_index("fsdp")
    t = lax.axis_index("tp")
    z = f // 8
    n = lax.rem(f, 8)
    g = n // 4
    role = lax.rem(lax.rem(n, 4) + 2 * lax.rem(t, 2), 4)
    lane = n * 4 + t
    slot = 4 * g + t

    def holder(plane, kind, group, half):
        return plane * 8 + half * 4 + lax.rem(kind + 2 * lax.rem(group, 2), 4)

    def remote(src, dst, send_sem, recv_sem, target):
        return pltpu.make_async_remote_copy(
            src_ref=src,
            dst_ref=dst,
            send_sem=send_sem,
            recv_sem=recv_sem,
            device_id=target,
            device_id_type=MESH,
        )

    def loop(count, body):
        def step(i, carry):
            body(i)
            return carry

        lax.fori_loop(0, count, step, 0)

    def taken(ref, sem):
        pltpu.make_async_copy(ref, ref, sem).wait()

    def weight_copies(kind, i):
        group, half = lax.rem(i, 4), i // 4
        layer = kind // 2
        target = (holder(z, kind, group, half), group)
        mine = (target[0] == f) & (group == t)
        columns = pl.ds(pl.multiple_of(group * 1024 + half * 512, 512), HALF)
        narrow = pl.ds(pl.multiple_of(group * HD, HD), HD)
        wide_to = slabs.at[lane, :, pl.ds(0, HALF)]
        narrow_to = slabs.at[lane, :, pl.ds(HALF, HD)]
        if kind % 2 == 0:
            pieces = (
                (None, new_wq.at[layer, :, columns], wide_to, 0),
                (half == 0, new_wk.at[layer, :, narrow], narrow_to, 1),
                (half == 1, new_wv.at[layer, :, narrow], narrow_to, 1),
            )
        else:
            pieces = ((None, new_wo.at[layer, :, columns], wide_to, 0),)
        return target, mine, pieces

    def send_weights(kind):
        def one(i):
            target, mine, pieces = weight_copies(kind, i)
            for cond, src, dst, k in pieces:
                here = mine if cond is None else mine & cond
                there = jnp.logical_not(mine) if cond is None else jnp.logical_not(mine) & cond

                @pl.when(there)
                def _():
                    remote(src, dst, w_send.at[kind, i, k], w_recv, target).start()

                @pl.when(here)
                def _():
                    pltpu.make_async_copy(src, dst, own_sem.at[k]).start()

        loop(8, one)

    def sent_weights(kind):
        def one(i):
            target, mine, pieces = weight_copies(kind, i)
            for cond, src, dst, k in pieces:
                there = jnp.logical_not(mine) if cond is None else jnp.logical_not(mine) & cond

                @pl.when(there)
                def _():
                    remote(src, dst, w_send.at[kind, i, k], w_recv, target).wait_send()

        loop(8, one)

    def x_copy(i):
        plane, half = i // 2, lax.rem(i, 2)
        target = (holder(plane, 0, t, half), t)
        src = x0_ref.at[:, pl.ds(pl.multiple_of(plane * PART, HD), PART)]
        copy = remote(src, x_land.at[f], x_send.at[i], x_recv, target)
        return target[0] != f, copy

    def r_copy(i):
        group = lax.rem(f // 4, 4)
        half = f // 16
        target = (holder(i, 2, group, half), group)
        src = xr_ref.at[:, pl.ds(pl.multiple_of(i * PART, HD), PART)]
        copy = remote(src, r_land.at[lax.rem(f, 4)], r_send.at[i], r_recv, target)
        return (group == t) & (target[0] != f), copy

    def b_copy(land, width, layer, i):
        src = product.at[i, :, pl.ds(0, width)]
        copy = remote(src, land.at[2 * z + g], b_send.at[i], b_recv.at[layer], (i, t))
        return i != f, copy

    def d_copy(layer, i):
        plane, half = i // 2, lax.rem(i, 2)
        target = (holder(plane, 2 * layer + 1, t, half), t)
        copy = remote(
            att.at[layer, half],
            d_land.at[layer, f],
            d_send.at[layer, i],
            d_recv.at[layer],
            target,
        )
        return target[0] != f, copy

    def e_copy(i):
        group, half = lax.rem(i, 4), i // 4
        target = (holder(z, 2, group, half), group)
        src = product.at[pl.ds(4 * i, 4), :, pl.ds(0, PART)]
        return remote(src, e_land.at[slot], e_send.at[i], e_recv, target)

    def ag_copy(i):
        group, half = lax.rem(i, 4), i // 4
        target = (holder(z, 2, group, half), group)
        copy = remote(ag_land.at[slot], ag_land.at[slot], ag_send.at[i], ag_recv, target)
        return i != slot, copy

    def h_copy(i):
        row_of = 4 * slot + i
        target = (z * 8 + lax.rem(row_of, 8), row_of // 8)
        copy = remote(h_keep.at[i], h_land, h_send.at[i], h_recv, target)
        return (target[0] != f) | (target[1] != t), copy

    def f_copy(i):
        target = (z * 8 + lax.rem(i, 8), i // 8)
        src = product.at[i, :, pl.ds(0, PART)]
        copy = remote(src, f_land.at[slot], f_send.at[i], f_recv, target)
        return (target[0] != f) | (target[1] != t), copy

    def o_copy(i):
        target = (8 * t + n, i)
        copy = remote(f_keep, o_land.at[z], o_send.at[i], o_recv, target)
        return (target[0] != f) | (target[1] != t), copy

    def start_all(count, make):
        def one(i):
            cond, copy = make(i)
            pl.when(cond)(copy.start)

        loop(count, one)

    def sent_all(count, make):
        def one(i):
            cond, copy = make(i)
            pl.when(cond)(copy.wait_send)

        loop(count, one)

    barrier = pltpu.get_barrier_semaphore()

    def greet(target):
        pl.semaphore_signal(barrier, inc=1, device_id=target, device_id_type=MESH)

    def greet_plane(i):
        other = lax.rem(lane + 1 + i, 32)
        greet((z * 8 + other // 4, lax.rem(other, 4)))

    def greet_group(i):
        greet((lax.rem(z + 1 + i // 8, 4) * 8 + lax.rem(i, 8), t))

    def greet_line(i):
        greet((lax.rem(z + 1 + i // 3, 4) * 8 + n, lax.rem(t + 1 + lax.rem(i, 3), 4)))

    loop(31, greet_plane)
    loop(24, greet_group)
    loop(9, greet_line)

    rows = pl.ds(pl.multiple_of(z * PART, HD), PART)
    half_cols = pl.ds(pl.multiple_of(g * HALF, HALF), HALF)

    def stale_copies(act):
        for kind in range(4):
            layer = kind // 2

            @pl.when(role == kind)
            def _():
                wide = old_wq if kind % 2 == 0 else old_wo
                act(
                    pltpu.make_async_copy(
                        wide.at[layer, rows, half_cols],
                        stale.at[:, pl.ds(0, HALF)],
                        local_sem.at[0],
                    )
                )
                if kind % 2 == 0:
                    for half, narrow in enumerate((old_wk, old_wv)):

                        @pl.when(g == half)
                        def _():
                            act(
                                pltpu.make_async_copy(
                                    narrow.at[layer, rows, :],
                                    stale.at[:, pl.ds(HALF, HD)],
                                    local_sem.at[1],
                                )
                            )

    stale_copies(lambda copy: copy.start())
    key_copy = pltpu.make_async_copy(cache_k, keys, local_sem.at[2])
    value_copy = pltpu.make_async_copy(cache_v, values, local_sem.at[3])
    key_copy.start()
    value_copy.start()

    pl.semaphore_wait(barrier, 64)

    send_weights(0)
    start_all(8, x_copy)

    @pl.when(role == 0)
    def _():
        x_land[f] = x0_ref[:, pl.ds(pl.multiple_of(z * PART, HD), PART)]

    send_weights(1)
    start_all(4, r_copy)

    @pl.when((role == 2) & (lax.rem(f // 4, 4) == t) & (f // 16 == g))
    def _():
        r_land[lax.rem(f, 4)] = xr_ref[:, pl.ds(pl.multiple_of(z * PART, HD), PART)]

    send_weights(2)
    send_weights(3)

    def prepare(width):
        used = pl.ds(0, width)
        taken(slabs.at[pl.ds(0, 31), :, used], w_recv)
        taken(slabs.at[0, :, pl.ds(0, HALF)], own_sem.at[0])
        if width > HALF:
            taken(slabs.at[0, :, pl.ds(HALF, HD)], own_sem.at[1])

        def pair(i):
            both = [slabs[2 * i + j, :, 0:width].astype(jnp.float32) for j in range(2)]
            raw[pl.ds(pl.multiple_of(40 * i, 8), 40), 0:width] = jnp.concatenate(both, axis=0)

        loop(16, pair)

        def block_row(i):
            at = pl.ds(pl.multiple_of(i * HD, HD), HD)
            for c in range(width // HD):
                cols = slice(c * HD, c * HD + HD)
                fresh[at, cols] = refresh_block(raw[at, cols])

        loop(5, block_row)
        stale_copies(lambda copy: copy.wait())

    def project(x, layer):
        chosen = use_new_rows(bound_ref, layer, ROWS)
        new = jnp.dot(x, fresh[...], preferred_element_type=jnp.float32)
        old = jnp.dot(x, stale[...], preferred_element_type=jnp.float32)
        product[:, :, 0:PART] = jnp.where(chosen, new, old).reshape(OWNERS, 8, PART)

    def out_project(layer):
        @pl.when(role == 2 * layer + 1)
        def _():
            d_land[layer, f] = att[layer, g]
            taken(d_land.at[layer, pl.ds(0, 31)], d_recv.at[layer])

        landed = d_land[layer].astype(jnp.float32)
        x = jnp.concatenate(
            [landed[:, 8 * h : 8 * h + 8, :].reshape(ROWS, HD) for h in range(4)], axis=1
        ).astype(jnp.bfloat16)
        chosen = use_new_rows(bound_ref, layer, ROWS)
        nt = (((1,), (1,)), ((), ()))
        new = lax.dot_general(x, fresh[:, 0:HALF], nt, preferred_element_type=jnp.float32)
        old = lax.dot_general(x, stale[:, 0:HALF], nt, preferred_element_type=jnp.float32)
        product[:, :, 0:PART] = jnp.where(chosen, new, old).reshape(OWNERS, 8, PART)

    def attention(layer, land, width):
        @pl.when(role == 2 * layer)
        def _():
            land[2 * z + g] = product[f, :, 0:width]
            taken(land.at[pl.ds(0, 7)], b_recv.at[layer])

        @pl.when(role != 2 * layer)
        def _():
            taken(land, b_recv.at[layer])

        sums = [sum(land[2 * plane + half] for plane in range(4)) for half in range(2)]
        if width > PART:
            inverse = lax.rsqrt(sums[0][:, PART : PART + 1] / D + 1e-06)
            sums = [part * inverse for part in sums]
        mixed = attend(
            sums, keys[layer].reshape(512, HD), values[layer].reshape(512, HD), length_ref
        )
        att[layer] = mixed.reshape(2, 32, HD)
        start_all(8, functools.partial(d_copy, layer))

    @pl.when(role == 0)
    def _():
        prepare(PART)
        taken(x_land.at[pl.ds(0, 31)], x_recv)
        project(x_land[...].reshape(ROWS, PART).astype(jnp.bfloat16), 0)
        start_all(OWNERS, functools.partial(b_copy, b0_land, PART, 0))

    @pl.when(role == 1)
    def _():
        prepare(HALF)

    key_copy.wait()
    value_copy.wait()
    attention(0, b0_land, PART)

    @pl.when(role == 1)
    def _():
        out_project(0)
        loop(8, lambda i: e_copy(i).start())

    @pl.when(role == 2)
    def _():
        prepare(PART)
        own_rows = (slot // 4 == f // 16) & (lax.rem(slot, 4) == lax.rem(f // 4, 4))

        @pl.when(own_rows)
        def _():
            taken(r_land.at[pl.ds(0, 3)], r_recv)

        @pl.when(jnp.logical_not(own_rows))
        def _():
            taken(r_land, r_recv)

        taken(e_land, e_recv)
        hidden = r_land[...]
        for other in range(8):
            hidden = hidden + e_land[other]
        h_keep[...] = hidden
        hidden = hidden.reshape(32, PART)
        square = jnp.sum(hidden * hidden, axis=1, keepdims=True)
        gain = gain_ref[:, pl.ds(pl.multiple_of(z * PART, HD), PART)]
        high = square.astype(jnp.bfloat16).astype(jnp.float32)
        first = lax.broadcasted_iota(jnp.int32, (32, HD), 1) < 64
        ag_land[slot, :, 0:PART] = (hidden * gain).astype(jnp.bfloat16)
        ag_land[slot, :, PART : PART + HD] = jnp.where(first, high, square - high).astype(
            jnp.bfloat16
        )
        start_all(8, ag_copy)
        start_all(4, h_copy)

        @pl.when(2 * t + g == slot)
        def _():
            h_land[...] = h_keep[lax.rem(n, 4)]

        taken(ag_land.at[pl.ds(0, 7)], ag_recv)
        everyone = ag_land[...].reshape(ROWS, PART + HD)
        project(everyone[:, 0:PART], 1)
        parts = everyone[:, PART : PART + HD].astype(jnp.float32)
        squares = parts[:, 0:1] + parts[:, 64:65]
        product[:, :, PART : PART + HD] = jnp.broadcast_to(squares, (ROWS, HD)).reshape(
            OWNERS, 8, HD
        )
        start_all(OWNERS, functools.partial(b_copy, b1_land, PART + HD, 1))

    @pl.when(role == 3)
    def _():
        prepare(HALF)

    attention(1, b1_land, PART + HD)

    @pl.when(role == 3)
    def _():
        out_project(1)
        start_all(OWNERS, f_copy)
        f_land[slot] = product[8 * t + n, :, 0:PART]
        taken(f_land.at[pl.ds(0, 7)], f_recv)

    @pl.when(role != 3)
    def _():
        taken(f_land, f_recv)

    @pl.when(jnp.logical_not((role == 2) & (2 * t + g == slot)))
    def _():
        taken(h_land, h_recv)

    final = h_land[...]
    for other in range(8):
        final = final + f_land[other]
    f_keep[...] = final
    start_all(4, o_copy)

    @pl.when(z == t)
    def _():
        o_land[z] = final
        taken(o_land.at[pl.ds(0, 3)], o_recv)

    @pl.when(z != t)
    def _():
        taken(o_land, o_recv)

    for plane in range(4):
        out_ref[:, plane * PART : plane * PART + PART] = o_land[plane]

    for kind in range(4):
        sent_weights(kind)
    sent_all(8, x_copy)
    sent_all(4, r_copy)
    sent_all(8, functools.partial(d_copy, 0))
    sent_all(8, functools.partial(d_copy, 1))
    sent_all(4, o_copy)

    @pl.when(role == 0)
    def _():
        sent_all(OWNERS, functools.partial(b_copy, b0_land, PART, 0))

    @pl.when(role == 1)
    def _():
        loop(8, lambda i: e_copy(i).wait_send())

    @pl.when(role == 2)
    def _():
        sent_all(8, ag_copy)
        sent_all(4, h_copy)
        sent_all(OWNERS, functools.partial(b_copy, b1_land, PART + HD, 1))

    @pl.when(role == 3)
    def _():
        sent_all(OWNERS, f_copy)


def normed(hidden, gain):
    mean_square = jnp.mean(hidden * hidden, axis=-1, keepdims=True)
    return (hidden * lax.rsqrt(mean_square + 1e-06) * gain.astype(jnp.float32)).astype(jnp.bfloat16)


def on_device(
    inputs,
    norm_gain,
    old_wq,
    old_wk,
    old_wv,
    old_wo,
    new_wq,
    new_wk,
    new_wv,
    new_wo,
    cache_keys,
    cache_values,
    cache_lengths,
    refresh_bound,
):
    entering = inputs.astype(jnp.float32).reshape(8, D)
    first = normed(entering, norm_gain[0]).astype(jnp.float32)
    gain = norm_gain[1:2].astype(jnp.float32)
    vmem = pl.BlockSpec(memory_space=pltpu.VMEM)
    smem = pl.BlockSpec(memory_space=pltpu.SMEM)
    hbm = pl.BlockSpec(memory_space=pl.ANY)
    f32, bf16 = jnp.float32, jnp.bfloat16
    dma = pltpu.SemaphoreType.DMA
    out = pl.pallas_call(
        kernel,
        out_shape=jax.ShapeDtypeStruct((8, D), f32),
        in_specs=[vmem] * 3 + [smem] * 2 + [hbm] * 10,
        out_specs=vmem,
        scratch_shapes=[
            pltpu.VMEM((32, KEEP, PART), bf16),
            pltpu.VMEM((PART, PART), f32),
            pltpu.VMEM((PART, PART), bf16),
            pltpu.VMEM((PART, PART), bf16),
            pltpu.VMEM((2, 2, 256, HD), bf16),
            pltpu.VMEM((2, 2, 256, HD), bf16),
            pltpu.VMEM((OWNERS, 8, PART), f32),
            pltpu.VMEM((4, 8, PART), f32),
            pltpu.VMEM((OWNERS, 8, PART + HD), f32),
            pltpu.VMEM((8, 8, PART), f32),
            pltpu.VMEM((8, 8, PART + HD), f32),
            pltpu.VMEM((2, 2, 32, HD), bf16),
            pltpu.VMEM((2, OWNERS, 32, HD), bf16),
            pltpu.VMEM((8, 4, 8, PART), f32),
            pltpu.VMEM((8, 32, PART + HD), bf16),
            pltpu.VMEM((4, 8, PART), f32),
            pltpu.VMEM((8, PART), f32),
            pltpu.VMEM((8, 8, PART), f32),
            pltpu.VMEM((8, PART), f32),
            pltpu.VMEM((4, 8, PART), f32),
            dma((4, 8, 2)),
            dma((8,)),
            dma((4,)),
            dma((OWNERS,)),
            dma((2, 8)),
            dma((8,)),
            dma((8,)),
            dma((4,)),
            dma((OWNERS,)),
            dma((4,)),
            dma,
            dma((2,)),
            dma((4,)),
            dma,
            dma,
            dma((2,)),
            dma((2,)),
            dma,
            dma,
            dma,
            dma,
            dma,
        ],
        compiler_params=pltpu.CompilerParams(
            collective_id=0, has_side_effects=True, vmem_limit_bytes=40 * 1024 * 1024
        ),
    )(
        first,
        entering,
        gain,
        cache_lengths,
        refresh_bound,
        old_wq,
        old_wk,
        old_wv,
        old_wo,
        new_wq,
        new_wk,
        new_wv,
        new_wo,
        cache_keys,
        cache_values,
    )
    return out.reshape(STEPS, 2, D)


def solution(mesh):
    in_specs = (
        P(None, "fsdp", None),
        P(),
        P(None, None, "tp"),
        P(None, None, "tp"),
        P(None, None, "tp"),
        P(None, None, "tp"),
        P(None, ("fsdp", "tp"), None),
        P(None, ("fsdp", "tp"), None),
        P(None, ("fsdp", "tp"), None),
        P(None, ("fsdp", "tp"), None),
        P(None, "fsdp", None, "tp"),
        P(None, "fsdp", None, "tp"),
        P("fsdp"),
        P(),
    )
    out_specs = P(None, "fsdp", None)
    return jax.shard_map(
        on_device, mesh=mesh, in_specs=in_specs, out_specs=out_specs, check_vma=False
    )
```
